32 devices in a mesh: groups: 2 (over y), expert: 4 (over z), dp: 4 (over x, core).
Axes of the slice: x: 2, y: 2, z: 4, core: 2. Of those that a mesh axis runs over, the one named last changes fastest.
Arguments:
- tokens: bfloat16 [128, 7168], P(('groups', 'expert', 'dp')), parts along dimension 0, may hold values from -6 to 6
- routes: int32 [128, 8], P(('groups', 'expert', 'dp')), parts along dimension 0, may hold values from 0 to 15, as said below
- combine_weight: bfloat16 [128, 8], P(('groups', 'expert', 'dp')), parts along dimension 0, may hold values from 0.049804688 to 0.59765625
- live_rows: int32 [32], P(('groups', 'expert', 'dp')), parts along dimension 0, may hold values from 1 to 4, as said below
- gate_projection_weight: bfloat16 [16, 7168, 2048], P('expert', None, 'dp'), may hold values from -0.0625 to 0.0625
- up_projection_weight: bfloat16 [16, 7168, 2048], P('expert', None, 'dp'), may hold values from -0.0625 to 0.0625
- down_projection_weight: bfloat16 [16, 2048, 7168], P('expert', 'dp'), may hold values from -0.125 to 0.125
Outputs:
- mixed: bfloat16 [128, 7168], P(('groups', 'expert', 'dp')), parts along dimension 0
The draws below stay inside these ranges and needn't reach their ends.
There are 2 independent parts, one for each index of `groups`. The reference program is written for one: setup_inputs(seed, part) draws one part's arguments, and reference() takes and returns one part's arrays. A program takes and returns all parts, laid end to end along the dimension named above; an argument that names none is the same for every part. Nothing has to cross between parts.
Inputs may be any that keep to these rules, and one draw needn't show every extreme that they name: `routes`: each row names 8 different experts; in each aligned block of 16 rows every expert is named by at least one row and no expert by more than 12 rows, and one expert by exactly 12. `live_rows`: entry i counts the live rows, the first ones, of the i-th block of 4 rows; all devices of some aligned block of 16 rows have all 4 rows live.
All inputs are finite; a program needn't handle non-finite values.
Results may differ from the reference program's by a relative error of at most 0.011.
Values may be sent and summed in bfloat16 or wider, within the bound.
A program may use at most 192 MiB of HBM per device.

```python
import jax
import jax.numpy as jnp
from jax import lax

D = 7168
FF = 2048
EXPERTS = 16
TOP = 8
TOK_DEV = 4
BLOCK_ROWS = 16
CAP = 12
TOKENS = 64
DEVS_PART = 16
FF_DEV = 512
N_EXPERT = 4
N_DP = 4


def draw_routes(key, part):
    key = jax.random.fold_in(key, 5)
    key_order, key_spread, key_rows, key_columns = jax.random.split(key, 4)
    block_count = TOKENS // BLOCK_ROWS
    mean_load = BLOCK_ROWS * TOP // EXPERTS
    half_load = mean_load // 2
    pair_count = EXPERTS // 2
    expert_order = jax.random.permutation(key_order, EXPERTS).astype(jnp.int32)
    pair_spread = jax.random.randint(key_spread, (block_count, pair_count), 0, half_load + 1, dtype=jnp.int32)
    pair_spread = pair_spread.at[:, 0].set(half_load)
    block_loads = jnp.concatenate([mean_load + pair_spread, mean_load - pair_spread[:, ::-1]], axis=1)
    load_ends = jnp.cumsum(block_loads, axis=1)
    slot_places = jnp.arange(BLOCK_ROWS * TOP, dtype=jnp.int32)
    run_rank = jnp.sum((load_ends[:, None, :] <= slot_places[None, :, None]).astype(jnp.int32), axis=2)
    named_expert = expert_order[run_rank]
    route_table = named_expert.reshape(block_count, TOP, BLOCK_ROWS).transpose(0, 2, 1)
    row_keys = jax.random.split(key_rows, block_count)
    row_shuffle = jax.vmap(lambda one_key: jax.random.permutation(one_key, BLOCK_ROWS))(row_keys).astype(jnp.int32)
    route_table = jnp.take_along_axis(route_table, row_shuffle[:, :, None], axis=1)
    route_table = route_table.reshape(TOKENS, TOP)
    column_keys = jax.random.split(key_columns, TOKENS)
    column_shuffle = jax.vmap(lambda one_key: jax.random.permutation(one_key, TOP))(column_keys).astype(jnp.int32)
    route_table = jnp.take_along_axis(route_table, column_shuffle, axis=1)
    return route_table.astype(jnp.int32)


def draw_live_rows(key, part):
    key = jax.random.fold_in(key, 11)
    first, second = jax.random.split(key)
    devices_block = BLOCK_ROWS // TOK_DEV
    block_count = DEVS_PART // devices_block
    values = jax.random.randint(first, (DEVS_PART,), 1, TOK_DEV + 1, dtype=jnp.int32)
    full_block = jax.random.randint(second, (), 0, block_count, dtype=jnp.int32)
    device_ids = jnp.arange(DEVS_PART, dtype=jnp.int32)
    is_full = device_ids // devices_block == full_block
    return jnp.where(is_full, jnp.int32(TOK_DEV), values).astype(jnp.int32)


def level_of(own_key, extent, pieces, least, top_value):
    loudness = 1.0
    for position, blocks in pieces:
        heights = jax.random.uniform(jax.random.fold_in(jax.random.fold_in(own_key, 6), position), (blocks,), jnp.float32, least / len(pieces), top_value / len(pieces))
        loudness = loudness * jnp.repeat(jnp.exp(heights), extent[position] // blocks).reshape((-1,) + (1,) * (len(extent) - 1 - position))
    return loudness


def bell_draw(key, dims, scale, most, cuts=(), kind=jnp.bfloat16):
    values = jax.random.normal(key, dims, jnp.float32) * scale
    if len(cuts) > 0:
        values = level_of(key, dims, cuts, -0.22, 0.18) * values
    return jnp.clip(values, min=-most, max=most).astype(kind)


def setup_inputs(seed: int = 0, part: int = 0) -> dict:
    key_of = jax.random.split(jax.random.key(seed), 8)
    part_keys = jax.random.split(jax.random.fold_in(key_of[7], part), 8)
    tokens = bell_draw(part_keys[0], (TOKENS, D), 1.0, 6.0, ((0, 16),))
    routes = draw_routes(jax.random.fold_in(jax.random.fold_in(key_of[7], part), 71), part)
    combine_weight = jnp.clip(0.049804688 + 0.54785156 * jax.random.uniform(part_keys[2], (TOKENS, TOP), jnp.float32) ** level_of(part_keys[2], (TOKENS, TOP), ((0, 16),), -0.2, 0.2), 0.049804688, 0.59765625).astype(jnp.bfloat16)
    live_rows = draw_live_rows(jax.random.fold_in(jax.random.fold_in(key_of[7], part), 71), part)
    gate_projection_weight = bell_draw(key_of[4], (EXPERTS, D, FF), D ** -0.5, 0.0625, ((0, 4), (2, 4)))
    up_projection_weight = bell_draw(key_of[5], (EXPERTS, D, FF), D ** -0.5, 0.0625, ((0, 4), (2, 4)))
    down_projection_weight = bell_draw(key_of[6], (EXPERTS, FF, D), FF ** -0.5, 0.125, ((0, 4), (1, 4)))
    return dict(tokens=tokens, routes=routes, combine_weight=combine_weight, live_rows=live_rows, gate_projection_weight=gate_projection_weight, up_projection_weight=up_projection_weight, down_projection_weight=down_projection_weight)


def expert_rows(rows, gate_block, up_block, down_block):
    gate_activation = jnp.dot(rows, gate_block, preferred_element_type=jnp.float32)
    upper_activation = jnp.dot(rows, up_block, preferred_element_type=jnp.float32)
    hidden_state = (jax.nn.silu(gate_activation) * upper_activation).astype(jnp.bfloat16)
    count = rows.shape[0]
    hidden_blocks = hidden_state.reshape(count, N_DP, FF_DEV).astype(jnp.float32)
    down_blocks = down_block.reshape(N_DP, FF_DEV, D).astype(jnp.float32)
    partial_value = jnp.einsum("rbf,bfd->brd", hidden_blocks, down_blocks)
    rounded = lax.optimization_barrier(partial_value.astype(jnp.bfloat16))
    return jnp.sum(rounded.astype(jnp.float32), axis=0).astype(jnp.bfloat16)


def reference(tokens, routes, combine_weight, live_rows, gate_projection_weight, up_projection_weight, down_projection_weight):
    row_ids = jnp.arange(TOKENS, dtype=jnp.int32)
    live_each = jnp.repeat(live_rows, TOK_DEV, total_repeat_length=TOKENS)
    valid_row = (row_ids % TOK_DEV) < live_each
    limit = N_EXPERT * CAP

    def one_expert(total, index):
        hit = (routes == index) & valid_row[:, None]
        chosen = jnp.any(hit, axis=1)
        weight = jnp.sum(jnp.where(hit, combine_weight.astype(jnp.float32), jnp.float32(0.0)), axis=1)
        order = jnp.argsort(jnp.where(chosen, 0, 1).astype(jnp.int32), stable=True)[:limit].astype(jnp.int32)
        rows = tokens[order]
        result = expert_rows(rows, gate_projection_weight[index], up_projection_weight[index], down_projection_weight[index])
        scale = weight[order] * chosen[order].astype(jnp.float32)
        total = total.at[order].add(scale[:, None] * result.astype(jnp.float32))
        return total, None

    start = jnp.zeros((TOKENS, D), jnp.float32)
    total, _ = lax.scan(one_expert, start, jnp.arange(EXPERTS, dtype=jnp.int32))
    return total.astype(jnp.bfloat16)
```

```python
import functools

import jax
import jax.numpy as jnp
from jax import lax
from jax.experimental import pallas as pl
from jax.experimental.pallas import tpu as pltpu
from jax.sharding import PartitionSpec as P

SLAB = 16
CHUNK = 512
LANES = 128
LAG = 2
MESH = pl.DeviceIdType.MESH


def kernel(
    n_x,
    n_z,
    depth,
    tokens,
    routes,
    combine,
    live,
    gate_w,
    up_w,
    down_w,
    out,
    gathered,
    rows,
    table,
    hidden,
    gate_acc,
    up_acc,
    gu_ring,
    down_buf,
    own_a,
    send_a,
    recv_a,
    own_x,
    send_x,
    recv_x,
    send_z,
    recv_z,
    gu_sem,
    down_sem,
    gz_send,
    gz_recv,
    gx_send,
    gx_recv,
    gc_send,
    gc_recv,
    a_ssem,
    a_rsem,
    x_ssem,
    x_rsem,
    z_ssem,
    z_rsem,
):
    f32, bf16 = jnp.float32, jnp.bfloat16
    tok, width = tokens.shape
    top = routes.shape[1]
    local_count, ff = gate_w.shape[0], gate_w.shape[2]
    quarters = SLAB // tok
    part = width // quarters
    count = width // CHUNK
    piece = CHUNK // quarters
    chip_rows = n_z * tok
    half = n_x * chip_rows
    total = 2 * half

    z = lax.axis_index("expert")
    dp = lax.axis_index("dp")
    core = lax.rem(dp, 2)
    x = lax.div(dp, 2)
    sibling = {"dp": x * 2 + 1 - core}

    def x_peer(dx):
        return {"dp": lax.rem(x + dx, n_x) * 2 + core}

    def z_peer(dz):
        return {"expert": lax.rem(z + dz, n_z)}

    def slab(c, dx, dz):
        return gathered.at[pl.ds(((c * n_x + dx) * n_z + dz) * SLAB, SLAB), :]

    barrier = pltpu.get_barrier_semaphore()
    peers = [sibling]
    peers += [x_peer(dx) for dx in range(1, n_x)]
    peers += [z_peer(dz) for dz in range(1, n_z)]
    for peer in peers:
        pl.semaphore_signal(barrier, inc=1, device_id=peer, device_id_type=MESH)

    def gu_copy(e, q, which):
        place = lax.rem(e, depth)
        return pltpu.make_async_copy(
            (gate_w, up_w)[which].at[e, pl.ds(q * part, part), :],
            gu_ring.at[place, q, which],
            gu_sem.at[place, q, which],
        )

    def down_copy(c):
        return pltpu.make_async_copy(
            down_w.at[:, :, pl.ds(pl.multiple_of(c * CHUNK, CHUNK), CHUNK)],
            down_buf.at[c],
            down_sem.at[c],
        )

    for e in range(depth):
        for q in range(quarters):
            for which in range(2):
                gu_copy(e, q, which).start()

    wide = tokens[...].astype(f32)
    packed = jnp.concatenate([wide[:, q * part : (q + 1) * part] for q in range(quarters)], axis=0)
    gathered[0:SLAB, 0:part] = packed.astype(bf16)
    lane = lax.broadcasted_iota(jnp.int32, (tok, LANES), 1)
    row = lax.broadcasted_iota(jnp.int32, (tok, LANES), 0)
    chosen = routes[...]
    share = combine[...].astype(f32)
    weights = jnp.zeros((tok, LANES), f32)
    for k in range(top):
        weights += jnp.where(chosen[:, k : k + 1] == lane, share[:, k : k + 1], 0.0)
    weights = jnp.where(row < live[0], weights, 0.0)
    gathered[0:SLAB, part : part + LANES] = jnp.concatenate([weights] * quarters, axis=0).astype(bf16)

    pl.semaphore_wait(barrier, len(peers))

    def gz(dz):
        return pltpu.make_async_remote_copy(
            src_ref=slab(0, 0, 0),
            dst_ref=slab(0, 0, n_z - dz),
            send_sem=gz_send.at[dz],
            recv_sem=gz_recv.at[n_z - dz],
            device_id=z_peer(dz),
            device_id_type=MESH,
        )

    def gx(dx, dz):
        return pltpu.make_async_remote_copy(
            src_ref=slab(0, 0, dz),
            dst_ref=slab(0, n_x - dx, dz),
            send_sem=gx_send.at[dx, dz],
            recv_sem=gx_recv.at[n_x - dx, dz],
            device_id=x_peer(dx),
            device_id_type=MESH,
        )

    def gc(dx, dz):
        return pltpu.make_async_remote_copy(
            src_ref=slab(0, dx, dz),
            dst_ref=slab(1, dx, dz),
            send_sem=gc_send.at[dx, dz],
            recv_sem=gc_recv.at[dx, dz],
            device_id=sibling,
            device_id_type=MESH,
        )

    order = sorted(range(1, n_z), key=lambda dz: (min(dz, n_z - dz), dz))
    for dz in order:
        gz(dz).start()
    for dz in [0] + order:
        if dz:
            gz(n_z - dz).wait_recv()
        for dx in range(1, n_x):
            gx(dx, dz).start()
        gc(0, dz).start()
    for dz in [0] + order:
        for dx in range(1, n_x):
            gx(n_x - dx, dz).wait_recv()
            gc(dx, dz).start()
    for dz in [0] + order:
        for dx in range(n_x):
            gc(dx, dz).wait_recv()
    for dz in range(n_z):
        if dz:
            gz(dz).wait_send()
        for dx in range(n_x):
            if dx:
                gx(dx, dz).wait_send()
            gc(dx, dz).wait_send()

    to = lax.broadcasted_iota(jnp.int32, (total, total * quarters), 0)
    came = lax.broadcasted_iota(jnp.int32, (total, total * quarters), 1)
    first = lax.div(to, tok) * SLAB + lax.rem(to, tok)
    for q in range(quarters):
        pick = jnp.where(came == first + q * tok, 1.0, 0.0).astype(bf16)
        rows[q] = jnp.dot(pick, gathered[:, 0:part], preferred_element_type=f32).astype(bf16)
        if q == 0:
            table[...] = jnp.dot(pick, gathered[:, part : part + LANES], preferred_element_type=f32)

    spread = -(-count // (depth * quarters))

    def expert(e, _):
        place = lax.rem(e, depth)
        for q in range(quarters):
            for which, acc in ((0, gate_acc), (1, up_acc)):
                gu_copy(e, q, which).wait()
                term = jnp.dot(rows[q], gu_ring[place, q, which], preferred_element_type=f32)
                if q == 0:
                    acc[...] = term
                else:
                    acc[...] += term

            @pl.when(e + depth < local_count)
            def _():
                for which in range(2):
                    gu_copy(e + depth, q, which).start()

            @pl.when(e + depth >= local_count)
            def _():
                begin = ((e + depth - local_count) * quarters + q) * spread
                for k in range(spread):

                    @pl.when(begin + k < count)
                    def _():
                        down_copy(begin + k).start()

        lanes = lax.broadcasted_iota(jnp.int32, (total, LANES), 1)
        mine = jnp.where(lanes == z * local_count + e, table[...], 0.0)
        weight = jnp.sum(mine, axis=1, keepdims=True)
        g = gate_acc[...]
        value = g / (1.0 + jnp.exp(-g)) * up_acc[...] * weight
        hidden[:, pl.ds(pl.multiple_of(e * ff, LANES), ff)] = value.astype(bf16)
        return 0

    lax.fori_loop(0, local_count, expert, 0)

    def cp_a(c):
        return pltpu.make_async_remote_copy(
            src_ref=send_a.at[c],
            dst_ref=recv_a.at[c],
            send_sem=a_ssem.at[c],
            recv_sem=a_rsem.at[c],
            device_id=sibling,
            device_id_type=MESH,
        )

    def cp_x(c, dx):
        return pltpu.make_async_remote_copy(
            src_ref=send_x.at[c, dx],
            dst_ref=recv_x.at[c, dx],
            send_sem=x_ssem.at[c, dx],
            recv_sem=x_rsem.at[c, dx],
            device_id=x_peer(dx),
            device_id_type=MESH,
        )

    def cp_z(c, dz):
        return pltpu.make_async_remote_copy(
            src_ref=send_z.at[c, dz],
            dst_ref=recv_z.at[c, dz],
            send_sem=z_ssem.at[c, dz],
            recv_sem=z_rsem.at[c, dz],
            device_id=z_peer(dz),
            device_id_type=MESH,
        )

    def project(c):
        down_copy(c).wait()
        down = down_buf[c].reshape(local_count * ff, CHUNK)
        y = jnp.dot(hidden[...], down, preferred_element_type=f32)
        send_a[c] = y[half:].astype(bf16)
        own_a[c] = y[:half]
        cp_a(c).start()

    def add_core(c):
        cp_a(c).wait_recv()
        y = own_a[c] + recv_a[c].astype(f32)
        own_x[c] = y[:chip_rows]
        for dx in range(1, n_x):
            send_x[c, dx] = y[dx * chip_rows : (dx + 1) * chip_rows].astype(bf16)
            cp_x(c, dx).start()

    put = lax.broadcasted_iota(jnp.int32, (n_z * SLAB, chip_rows), 0)
    take = lax.broadcasted_iota(jnp.int32, (n_z * SLAB, chip_rows), 1)
    source = lax.div(put, SLAB) * tok + lax.rem(put, tok)
    block = lax.rem(lax.div(put, tok), quarters)

    def add_x(c):
        y = own_x[c]
        for dx in range(1, n_x):
            cp_x(c, dx).wait_recv()
            y += recv_x[c, dx].astype(f32)
        y = y.astype(bf16)
        slabs = jnp.zeros((n_z * SLAB, piece), f32)
        for q in range(quarters):
            pick = jnp.where((take == source) & (block == q), 1.0, 0.0).astype(bf16)
            slabs += jnp.dot(pick, y[:, q * piece : (q + 1) * piece], preferred_element_type=f32)
        send_z[c] = slabs.astype(bf16).reshape(n_z, SLAB, piece)
        for dz in range(1, n_z):
            cp_z(c, dz).start()

    def finish(c):
        y = send_z[c, 0].astype(f32)
        for dz in range(1, n_z):
            cp_z(c, dz).wait_recv()
            y += recv_z[c, dz].astype(f32)
        for q in range(quarters):
            at = pl.multiple_of(c * CHUNK + q * piece, LANES)
            out[:, pl.ds(at, piece)] = y[q * tok : (q + 1) * tok].astype(bf16)

    def step(i, _):
        for lag, stage in ((0, project), (LAG, add_core), (2 * LAG, add_x), (3 * LAG, finish)):

            @pl.when((i >= lag) & (i < count + lag))
            def _():
                stage(i - lag)

        return 0

    lax.fori_loop(0, count + 3 * LAG, step, 0)

    def drain(c, _):
        cp_a(c).wait_send()
        for dx in range(1, n_x):
            cp_x(c, dx).wait_send()
        for dz in range(1, n_z):
            cp_z(c, dz).wait_send()
        return 0

    lax.fori_loop(0, count, drain, 0)


def body(
    tokens,
    routes,
    combine_weight,
    live_rows,
    gate_projection_weight,
    up_projection_weight,
    down_projection_weight,
):
    f32, bf16 = jnp.float32, jnp.bfloat16
    tok, width = tokens.shape
    n_dp = lax.axis_size("dp")
    n_z = lax.axis_size("expert")
    n_x = n_dp // 2
    local_count, _, ff = gate_projection_weight.shape
    quarters = SLAB // tok
    part = width // quarters
    count = width // CHUNK
    piece = CHUNK // quarters
    chip_rows = n_z * tok
    half = n_x * chip_rows
    total = 2 * half
    depth = min(2, local_count)
    vmem = pl.BlockSpec(memory_space=pltpu.VMEM)
    smem = pl.BlockSpec(memory_space=pltpu.SMEM)
    hbm = pl.BlockSpec(memory_space=pl.ANY)
    sem = pltpu.SemaphoreType.DMA
    weights = 3 * local_count * width * ff
    return pl.pallas_call(
        functools.partial(kernel, n_x, n_z, depth),
        out_shape=jax.ShapeDtypeStruct((tok, width), bf16),
        in_specs=[vmem, vmem, vmem, smem, hbm, hbm, hbm],
        out_specs=vmem,
        scratch_shapes=[
            pltpu.VMEM((total * quarters, part + LANES), bf16),
            pltpu.VMEM((quarters, total, part), bf16),
            pltpu.VMEM((total, LANES), f32),
            pltpu.VMEM((total, local_count * ff), bf16),
            pltpu.VMEM((total, ff), f32),
            pltpu.VMEM((total, ff), f32),
            pltpu.VMEM((depth, quarters, 2, part, ff), bf16),
            pltpu.VMEM((count, local_count, ff, CHUNK), bf16),
            pltpu.VMEM((count, half, CHUNK), f32),
            pltpu.VMEM((count, half, CHUNK), bf16),
            pltpu.VMEM((count, half, CHUNK), bf16),
            pltpu.VMEM((count, chip_rows, CHUNK), f32),
            pltpu.VMEM((count, n_x, chip_rows, CHUNK), bf16),
            pltpu.VMEM((count, n_x, chip_rows, CHUNK), bf16),
            pltpu.VMEM((count, n_z, SLAB, piece), bf16),
            pltpu.VMEM((count, n_z, SLAB, piece), bf16),
            sem((depth, quarters, 2)),
            sem((count,)),
            sem((n_z,)),
            sem((n_z,)),
            sem((n_x, n_z)),
            sem((n_x, n_z)),
            sem((n_x, n_z)),
            sem((n_x, n_z)),
            sem((count,)),
            sem((count,)),
            sem((count, n_x)),
            sem((count, n_x)),
            sem((count, n_z)),
            sem((count, n_z)),
        ],
        compiler_params=pltpu.CompilerParams(
            collective_id=0, has_side_effects=True, vmem_limit_bytes=64 * 1024 * 1024 - 65536
        ),
        cost_estimate=pl.CostEstimate(
            flops=2 * total * weights, bytes_accessed=2 * weights, transcendentals=total * ff * local_count
        ),
    )(
        tokens,
        routes,
        combine_weight,
        live_rows,
        gate_projection_weight,
        up_projection_weight,
        down_projection_weight,
    )


def solution(mesh):
    placed = (
        P(("groups", "expert", "dp"), None),
        P(("groups", "expert", "dp"), None),
        P(("groups", "expert", "dp"), None),
        P(("groups", "expert", "dp")),
        P("expert", None, "dp"),
        P("expert", None, "dp"),
        P("expert", "dp", None),
    )
    return jax.shard_map(
        body,
        mesh=mesh,
        in_specs=placed,
        out_specs=P(("groups", "expert", "dp"), None),
        check_vma=False,
    )
```

```python
import functools

import jax
import jax.numpy as jnp
from jax import lax
from jax.experimental import pallas as pl
from jax.experimental.pallas import tpu as pltpu
from jax.sharding import PartitionSpec as P

SLAB = 16
CHUNK = 1024
HALVES = 2
BITES = 2
LANES = 128
LAG = 2
MESH = pl.DeviceIdType.MESH


def kernel(
    n_x,
    n_z,
    depth,
    tokens_hbm,
    routes_hbm,
    combine_hbm,
    live_hbm,
    gate_w,
    up_w,
    down_w,
    out,
    tokens,
    routes,
    combine,
    live,
    gathered_0,
    gathered_1,
    rows,
    table,
    hidden,
    acc,
    gu_ring,
    down_buf,
    own_a,
    send_a,
    recv_a,
    send_z,
    recv_z,
    in_sem,
    gu_sem,
    down_sem,
    gz_send,
    gz_recv,
    gx_send,
    gx_recv,
    gc_send,
    gc_recv,
    a_ssem,
    a_rsem,
    z_ssem,
    z_rsem,
):
    f32, bf16 = jnp.float32, jnp.bfloat16
    tok, width = tokens.shape
    top = routes.shape[1]
    local_count, ff = gate_w.shape[0], gate_w.shape[2]
    groups = SLAB // tok
    deep = width // HALVES
    part = deep // groups
    bite = deep // BITES
    count = width // CHUNK
    piece = CHUNK // groups
    chip_rows = n_z * tok
    total = 2 * n_x * chip_rows
    units = HALVES * local_count

    z = lax.axis_index("expert")
    dp = lax.axis_index("dp")
    core = lax.rem(dp, 2)
    x = lax.div(dp, 2)

    def dp_peer(c, dx):
        place = lax.rem(x + dx, n_x) * 2
        return {"dp": place + (1 - core if c else core)}

    def z_peer(dz):
        return {"expert": lax.rem(z + dz, n_z)}

    def slab(h, c, dx, dz):
        at = pl.ds(((c * n_x + dx) * n_z + dz) * SLAB, SLAB)
        return (gathered_0, gathered_1)[h].at[at, :]

    barrier = pltpu.get_barrier_semaphore()
    others = [(c, dx) for dx in range(n_x) for c in range(2) if c or dx]
    peers = [dp_peer(c, dx) for c, dx in others]
    peers += [z_peer(dz) for dz in range(1, n_z)]
    for peer in peers:
        pl.semaphore_signal(barrier, inc=1, device_id=peer, device_id_type=MESH)

    inputs = [
        pltpu.make_async_copy(source, target, in_sem.at[i])
        for i, (source, target) in enumerate(
            (
                (tokens_hbm, tokens),
                (routes_hbm, routes),
                (combine_hbm, combine),
                (live_hbm, live),
            )
        )
    ]
    for copy in inputs:
        copy.start()

    def gu_copy(t, b, which):
        place = lax.rem(t, depth)
        h = lax.div(t, local_count)
        e = lax.rem(t, local_count)
        begin = pl.multiple_of(h * deep + b * bite, SLAB)
        return pltpu.make_async_copy(
            (gate_w, up_w)[which].at[e, pl.ds(begin, bite), :],
            gu_ring.at[place, which, b],
            gu_sem.at[place, which, b],
        )

    def down_copy(c):
        return pltpu.make_async_copy(
            down_w.at[:, :, pl.ds(pl.multiple_of(c * CHUNK, CHUNK), CHUNK)],
            down_buf.at[c],
            down_sem.at[c],
        )

    for t in range(depth):
        for b in range(BITES):
            for which in range(2):
                gu_copy(t, b, which).start()

    for copy in inputs:
        copy.wait()

    wide = tokens[...].astype(f32)
    for h, target in enumerate((gathered_0, gathered_1)):
        cut = [wide[:, h * deep + g * part : h * deep + (g + 1) * part] for g in range(groups)]
        target[0:SLAB, 0:part] = jnp.concatenate(cut, axis=0).astype(bf16)
    lane = lax.broadcasted_iota(jnp.int32, (tok, LANES), 1)
    row = lax.broadcasted_iota(jnp.int32, (tok, LANES), 0)
    chosen = routes[...]
    share = combine[...].astype(f32)
    weights = jnp.zeros((tok, LANES), f32)
    for k in range(top):
        weights += jnp.where(chosen[:, k : k + 1] == lane, share[:, k : k + 1], 0.0)
    weights = jnp.where(row < live[...], weights, 0.0)
    gathered_0[0:SLAB, part : part + LANES] = jnp.concatenate([weights] * groups, axis=0).astype(bf16)

    pl.semaphore_wait(barrier, len(peers))

    def gz(h, dz):
        return pltpu.make_async_remote_copy(
            src_ref=slab(h, 0, 0, 0),
            dst_ref=slab(h, 0, 0, n_z - dz),
            send_sem=gz_send.at[h, dz],
            recv_sem=gz_recv.at[h, n_z - dz],
            device_id=z_peer(dz),
            device_id_type=MESH,
        )

    def gx(h, dx, dz):
        return pltpu.make_async_remote_copy(
            src_ref=slab(h, 0, 0, dz),
            dst_ref=slab(h, 0, n_x - dx, dz),
            send_sem=gx_send.at[h, dx, dz],
            recv_sem=gx_recv.at[h, n_x - dx, dz],
            device_id=dp_peer(0, dx),
            device_id_type=MESH,
        )

    def gc(h, dx, dz):
        return pltpu.make_async_remote_copy(
            src_ref=slab(h, 0, dx, dz),
            dst_ref=slab(h, 1, dx, dz),
            send_sem=gc_send.at[h, dx, dz],
            recv_sem=gc_recv.at[h, dx, dz],
            device_id=dp_peer(1, 0),
            device_id_type=MESH,
        )

    order = sorted(range(1, n_z), key=lambda dz: (min(dz, n_z - dz), dz))

    def spread_z(h):
        for dz in order:
            gz(h, dz).start()
        for dx in range(1, n_x):
            gx(h, dx, 0).start()
        gc(h, 0, 0).start()

    def spread_x(h):
        for dz in order:
            gz(h, n_z - dz).wait_recv()
            for dx in range(1, n_x):
                gx(h, dx, dz).start()
            gc(h, 0, dz).start()

    def spread_core(h):
        for dz in [0] + order:
            for dx in range(1, n_x):
                gx(h, n_x - dx, dz).wait_recv()
                gc(h, dx, dz).start()

    def whole_rows(h):
        for dz in [0] + order:
            for dx in range(n_x):
                gc(h, dx, dz).wait_recv()
        to = lax.broadcasted_iota(jnp.int32, (total, total * groups), 0)
        came = lax.broadcasted_iota(jnp.int32, (total, total * groups), 1)
        first = lax.div(to, tok) * SLAB + lax.rem(to, tok)
        source = (gathered_0, gathered_1)[h]
        for g in range(groups):
            pick = jnp.where(came == first + g * tok, 1.0, 0.0).astype(bf16)
            if g == 0 and h == 0:
                both = jnp.dot(pick, source[...], preferred_element_type=f32)
                table[...] = both[:, part:]
                both = both[:, :part]
            else:
                both = jnp.dot(pick, source[:, :part], preferred_element_type=f32)
            rows[h, :, g * part : (g + 1) * part] = both.astype(bf16)

    steps = min(depth, units) * BITES
    spread = -(-count // steps)

    def multiply(h, e):
        t = h * local_count + e
        place = lax.rem(t, depth)
        for b in range(BITES):
            for which in range(2):
                gu_copy(t, b, which).wait()
                term = jnp.dot(
                    rows[h, :, b * bite : (b + 1) * bite],
                    gu_ring[place, which, b],
                    preferred_element_type=f32,
                )
                if b == 0 and h == 0:
                    acc[e, which] = term
                else:
                    acc[e, which] += term

            @pl.when(t + depth < units)
            def _():
                for which in range(2):
                    gu_copy(t + depth, b, which).start()

            @pl.when(t + depth >= units)
            def _():
                begin = ((t + depth - units) * BITES + b) * spread
                for k in range(spread):

                    @pl.when(begin + k < count)
                    def _():
                        down_copy(begin + k).start()

    def activate(e):
        lanes = lax.broadcasted_iota(jnp.int32, (total, LANES), 1)
        mine = jnp.where(lanes == z * local_count + e, table[...], 0.0)
        weight = jnp.sum(mine, axis=1, keepdims=True)
        g = acc[e, 0]
        value = g / (1.0 + jnp.exp(-g)) * acc[e, 1] * weight
        hidden[:, pl.ds(pl.multiple_of(e * ff, LANES), ff)] = value.astype(bf16)

    spread_z(0)
    spread_x(0)
    spread_z(1)
    spread_core(0)
    whole_rows(0)

    def first_half(e, _):
        multiply(0, e)

        @pl.when(e == 0)
        def _():
            spread_x(1)

        @pl.when(e == min(1, local_count - 1))
        def _():
            spread_core(1)

        return 0

    lax.fori_loop(0, local_count, first_half, 0)
    whole_rows(1)

    def second_half(e, _):
        multiply(1, e)
        activate(e)
        return 0

    lax.fori_loop(0, local_count, second_half, 0)

    def cp_a(c, i):
        return pltpu.make_async_remote_copy(
            src_ref=send_a.at[c, i],
            dst_ref=recv_a.at[c, i],
            send_sem=a_ssem.at[c, i],
            recv_sem=a_rsem.at[c, i],
            device_id=dp_peer(*others[i]),
            device_id_type=MESH,
        )

    def cp_z(c, dz):
        return pltpu.make_async_remote_copy(
            src_ref=send_z.at[c, dz],
            dst_ref=recv_z.at[c, dz],
            send_sem=z_ssem.at[c, dz],
            recv_sem=z_rsem.at[c, dz],
            device_id=z_peer(dz),
            device_id_type=MESH,
        )

    def project(c):
        down_copy(c).wait()
        down = down_buf[c].reshape(local_count * ff, CHUNK)
        y = jnp.dot(hidden[...], down, preferred_element_type=f32)
        own_a[c] = y[:chip_rows]
        for i, (k, dx) in enumerate(others):
            at = (k * n_x + dx) * chip_rows
            send_a[c, i] = y[at : at + chip_rows].astype(bf16)
        for i in reversed(range(len(others))):
            cp_a(c, i).start()

    def add_dp(c):
        y = own_a[c]
        for i in range(len(others)):
            cp_a(c, i).wait_recv()
            y += recv_a[c, i].astype(f32)
        for dz in range(n_z):
            cut = y[dz * tok : (dz + 1) * tok]
            cut = [cut[:, g * piece : (g + 1) * piece] for g in range(groups)]
            send_z[c, dz] = jnp.concatenate(cut, axis=0).astype(bf16)
        for dz in order:
            cp_z(c, dz).start()

    def finish(c):
        y = send_z[c, 0].astype(f32)
        for dz in range(1, n_z):
            cp_z(c, dz).wait_recv()
            y += recv_z[c, dz].astype(f32)
        for g in range(groups):
            at = pl.multiple_of(c * CHUNK + g * piece, LANES)
            out[:, pl.ds(at, piece)] = y[g * tok : (g + 1) * tok].astype(bf16)

    def step(i, _):
        for lag, stage in ((0, project), (LAG, add_dp), (2 * LAG, finish)):

            @pl.when((i >= lag) & (i < count + lag))
            def _():
                stage(i - lag)

        return 0

    lax.fori_loop(0, count + 2 * LAG, step, 0)

    for h in range(HALVES):
        for dz in range(n_z):
            if dz:
                gz(h, dz).wait_send()
            for dx in range(n_x):
                if dx:
                    gx(h, dx, dz).wait_send()
                gc(h, dx, dz).wait_send()

    def drain(c, _):
        for i in range(len(others)):
            cp_a(c, i).wait_send()
        for dz in range(1, n_z):
            cp_z(c, dz).wait_send()
        return 0

    lax.fori_loop(0, count, drain, 0)


def body(
    tokens,
    routes,
    combine_weight,
    live_rows,
    gate_projection_weight,
    up_projection_weight,
    down_projection_weight,
):
    f32, bf16 = jnp.float32, jnp.bfloat16
    tok, width = tokens.shape
    top = routes.shape[1]
    n_dp = lax.axis_size("dp")
    n_z = lax.axis_size("expert")
    n_x = n_dp // 2
    local_count, _, ff = gate_projection_weight.shape
    groups = SLAB // tok
    deep = width // HALVES
    part = deep // groups
    count = width // CHUNK
    piece = CHUNK // groups
    chip_rows = n_z * tok
    total = n_dp * chip_rows
    depth = min(4, HALVES * local_count)
    vmem = pl.BlockSpec(memory_space=pltpu.VMEM)
    hbm = pl.BlockSpec(memory_space=pl.ANY)
    sem = pltpu.SemaphoreType.DMA
    weights = 3 * local_count * width * ff
    return pl.pallas_call(
        functools.partial(kernel, n_x, n_z, depth),
        out_shape=jax.ShapeDtypeStruct((tok, width), bf16),
        in_specs=[hbm] * 7,
        out_specs=vmem,
        scratch_shapes=[
            pltpu.VMEM((tok, width), bf16),
            pltpu.VMEM((tok, top), jnp.int32),
            pltpu.VMEM((tok, top), bf16),
            pltpu.VMEM((1, 1), jnp.int32),
            pltpu.VMEM((total * groups, part + LANES), bf16),
            pltpu.VMEM((total * groups, part), bf16),
            pltpu.VMEM((HALVES, total, deep), bf16),
            pltpu.VMEM((total, LANES), f32),
            pltpu.VMEM((total, local_count * ff), bf16),
            pltpu.VMEM((local_count, 2, total, ff), f32),
            pltpu.VMEM((depth, 2, BITES, deep // BITES, ff), bf16),
            pltpu.VMEM((count, local_count, ff, CHUNK), bf16),
            pltpu.VMEM((count, chip_rows, CHUNK), f32),
            pltpu.VMEM((count, n_dp - 1, chip_rows, CHUNK), bf16),
            pltpu.VMEM((count, n_dp - 1, chip_rows, CHUNK), bf16),
            pltpu.VMEM((count, n_z, SLAB, piece), bf16),
            pltpu.VMEM((count, n_z, SLAB, piece), bf16),
            sem((4,)),
            sem((depth, 2, BITES)),
            sem((count,)),
            sem((HALVES, n_z)),
            sem((HALVES, n_z)),
            sem((HALVES, n_x, n_z)),
            sem((HALVES, n_x, n_z)),
            sem((HALVES, n_x, n_z)),
            sem((HALVES, n_x, n_z)),
            sem((count, n_dp - 1)),
            sem((count, n_dp - 1)),
            sem((count, n_z)),
            sem((count, n_z)),
        ],
        compiler_params=pltpu.CompilerParams(
            collective_id=0, has_side_effects=True, vmem_limit_bytes=64 * 1024 * 1024 - 65536
        ),
        cost_estimate=pl.CostEstimate(
            flops=2 * total * weights, bytes_accessed=2 * weights, transcendentals=total * ff * local_count
        ),
    )(
        tokens,
        routes,
        combine_weight,
        live_rows.reshape(1, 1),
        gate_projection_weight,
        up_projection_weight,
        down_projection_weight,
    )


def solution(mesh):
    placed = (
        P(("groups", "expert", "dp"), None),
        P(("groups", "expert", "dp"), None),
        P(("groups", "expert", "dp"), None),
        P(("groups", "expert", "dp")),
        P("expert", None, "dp"),
        P("expert", None, "dp"),
        P("expert", "dp", None),
    )
    return jax.shard_map(
        body,
        mesh=mesh,
        in_specs=placed,
        out_specs=P(("groups", "expert", "dp"), None),
        check_vma=False,
    )
```

```python
import functools

import jax
import jax.numpy as jnp
from jax import lax
from jax.experimental import pallas as pl
from jax.experimental.pallas import tpu as pltpu
from jax.sharding import PartitionSpec as P

SLAB = 16
CHUNK = 1024
HALVES = 2
BITES = 2
LANES = 128
LAGS = (0, 2, 5, 8)
MESH = pl.DeviceIdType.MESH


def kernel(
    n_x,
    n_z,
    depth,
    tokens_hbm,
    routes_hbm,
    combine_hbm,
    live_hbm,
    gate_w,
    up_w,
    down_w,
    out,
    tokens,
    routes,
    combine,
    live,
    gathered_0,
    gathered_1,
    rows,
    table,
    hidden,
    acc,
    gu_ring,
    down_buf,
    own_a,
    send_a,
    recv_a,
    send_x,
    recv_x,
    send_z,
    recv_z,
    in_sem,
    gu_sem,
    down_sem,
    gz_send,
    gz_recv,
    gx_send,
    gx_recv,
    gc_send,
    gc_recv,
    a_ssem,
    a_rsem,
    x_ssem,
    x_rsem,
    z_ssem,
    z_rsem,
):
    f32, bf16 = jnp.float32, jnp.bfloat16
    tok, width = tokens.shape
    top = routes.shape[1]
    local_count, ff = gate_w.shape[0], gate_w.shape[2]
    groups = SLAB // tok
    deep = width // HALVES
    part = deep // groups
    bite = deep // BITES
    count = width // CHUNK
    piece = CHUNK // groups
    chip_rows = n_z * tok
    half = n_x * chip_rows
    total = 2 * half
    units = HALVES * local_count

    z = lax.axis_index("expert")
    dp = lax.axis_index("dp")
    core = lax.rem(dp, 2)
    x = lax.div(dp, 2)

    def dp_peer(c, dx):
        place = lax.rem(x + dx, n_x) * 2
        return {"dp": place + (1 - core if c else core)}

    def z_peer(dz):
        return {"expert": lax.rem(z + dz, n_z)}

    def slab(h, c, dx, dz):
        at = pl.ds(((c * n_x + dx) * n_z + dz) * SLAB, SLAB)
        return (gathered_0, gathered_1)[h].at[at, :]

    barrier = pltpu.get_barrier_semaphore()
    peers = [dp_peer(1, 0)]
    peers += [dp_peer(0, dx) for dx in range(1, n_x)]
    peers += [z_peer(dz) for dz in range(1, n_z)]
    for peer in peers:
        pl.semaphore_signal(barrier, inc=1, device_id=peer, device_id_type=MESH)

    inputs = [
        pltpu.make_async_copy(source, target, in_sem.at[i])
        for i, (source, target) in enumerate(
            (
                (tokens_hbm, tokens),
                (routes_hbm, routes),
                (combine_hbm, combine),
                (live_hbm, live),
            )
        )
    ]
    for copy in inputs:
        copy.start()

    def gu_copy(t, b, which):
        place = lax.rem(t, depth)
        h = lax.div(t, local_count)
        e = lax.rem(t, local_count)
        begin = pl.multiple_of(h * deep + b * bite, SLAB)
        return pltpu.make_async_copy(
            (gate_w, up_w)[which].at[e, pl.ds(begin, bite), :],
            gu_ring.at[place, which, b],
            gu_sem.at[place, which, b],
        )

    def down_copy(c):
        return pltpu.make_async_copy(
            down_w.at[:, :, pl.ds(pl.multiple_of(c * CHUNK, CHUNK), CHUNK)],
            down_buf.at[c],
            down_sem.at[c],
        )

    for t in range(depth):
        for b in range(BITES):
            for which in range(2):
                gu_copy(t, b, which).start()

    for copy in inputs:
        copy.wait()

    wide = tokens[...].astype(f32)
    for h, target in enumerate((gathered_0, gathered_1)):
        cut = [wide[:, h * deep + g * part : h * deep + (g + 1) * part] for g in range(groups)]
        target[0:SLAB, 0:part] = jnp.concatenate(cut, axis=0).astype(bf16)
    lane = lax.broadcasted_iota(jnp.int32, (tok, LANES), 1)
    row = lax.broadcasted_iota(jnp.int32, (tok, LANES), 0)
    chosen = routes[...]
    share = combine[...].astype(f32)
    weights = jnp.zeros((tok, LANES), f32)
    for k in range(top):
        weights += jnp.where(chosen[:, k : k + 1] == lane, share[:, k : k + 1], 0.0)
    weights = jnp.where(row < live[...], weights, 0.0)
    gathered_0[0:SLAB, part : part + LANES] = jnp.concatenate([weights] * groups, axis=0).astype(bf16)

    pl.semaphore_wait(barrier, len(peers))

    def gz(h, dz):
        return pltpu.make_async_remote_copy(
            src_ref=slab(h, 0, 0, 0),
            dst_ref=slab(h, 0, 0, n_z - dz),
            send_sem=gz_send.at[h, dz],
            recv_sem=gz_recv.at[h, n_z - dz],
            device_id=z_peer(dz),
            device_id_type=MESH,
        )

    def gx(h, dx, dz):
        return pltpu.make_async_remote_copy(
            src_ref=slab(h, 0, 0, dz),
            dst_ref=slab(h, 0, n_x - dx, dz),
            send_sem=gx_send.at[h, dx, dz],
            recv_sem=gx_recv.at[h, n_x - dx, dz],
            device_id=dp_peer(0, dx),
            device_id_type=MESH,
        )

    def gc(h, dx, dz):
        return pltpu.make_async_remote_copy(
            src_ref=slab(h, 0, dx, dz),
            dst_ref=slab(h, 1, dx, dz),
            send_sem=gc_send.at[h, dx, dz],
            recv_sem=gc_recv.at[h, dx, dz],
            device_id=dp_peer(1, 0),
            device_id_type=MESH,
        )

    order = sorted(range(1, n_z), key=lambda dz: (min(dz, n_z - dz), dz))

    def spread_z(h):
        for dz in order:
            gz(h, dz).start()
        for dx in range(1, n_x):
            gx(h, dx, 0).start()
        gc(h, 0, 0).start()

    def spread_x(h):
        for dz in order:
            gz(h, n_z - dz).wait_recv()
            for dx in range(1, n_x):
                gx(h, dx, dz).start()
            gc(h, 0, dz).start()

    def spread_core(h):
        for dz in [0] + order:
            for dx in range(1, n_x):
                gx(h, n_x - dx, dz).wait_recv()
                gc(h, dx, dz).start()

    def whole_rows(h):
        for dz in [0] + order:
            for dx in range(n_x):
                gc(h, dx, dz).wait_recv()
        to = lax.broadcasted_iota(jnp.int32, (total, total * groups), 0)
        came = lax.broadcasted_iota(jnp.int32, (total, total * groups), 1)
        within = to & (tok - 1)
        first = (to - within) * groups + within
        source = (gathered_0, gathered_1)[h]
        for g in range(groups):
            pick = jnp.where(came == first + g * tok, 1.0, 0.0).astype(bf16)
            if g == 0 and h == 0:
                both = jnp.dot(pick, source[...], preferred_element_type=f32)
                table[...] = both[:, part:]
                both = both[:, :part]
            else:
                both = jnp.dot(pick, source[:, :part], preferred_element_type=f32)
            rows[h, :, g * part : (g + 1) * part] = both.astype(bf16)

    steps = min(depth, units) * BITES
    spread = -(-count // steps)

    def multiply(h, e):
        t = h * local_count + e
        place = lax.rem(t, depth)
        for b in range(BITES):
            for which in range(2):
                gu_copy(t, b, which).wait()
                term = jnp.dot(
                    rows[h, :, b * bite : (b + 1) * bite],
                    gu_ring[place, which, b],
                    preferred_element_type=f32,
                )
                if b == 0 and h == 0:
                    acc[e, which] = term
                else:
                    acc[e, which] += term

            @pl.when(t + depth < units)
            def _():
                for which in range(2):
                    gu_copy(t + depth, b, which).start()

            @pl.when(t + depth >= units)
            def _():
                begin = ((t + depth - units) * BITES + b) * spread
                for k in range(spread):

                    @pl.when(begin + k < count)
                    def _():
                        down_copy(begin + k).start()

    def activate(e):
        lanes = lax.broadcasted_iota(jnp.int32, (total, LANES), 1)
        mine = jnp.where(lanes == z * local_count + e, table[...], 0.0)
        weight = jnp.sum(mine, axis=1, keepdims=True)
        g = acc[e, 0]
        value = g / (1.0 + jnp.exp(-g)) * acc[e, 1] * weight
        hidden[:, pl.ds(pl.multiple_of(e * ff, LANES), ff)] = value.astype(bf16)

    spread_z(0)
    spread_x(0)
    spread_z(1)
    spread_core(0)
    whole_rows(0)

    def first_half(e, _):
        multiply(0, e)

        @pl.when(e == 0)
        def _():
            spread_x(1)

        @pl.when(e == min(1, local_count - 1))
        def _():
            spread_core(1)

        return 0

    lax.fori_loop(0, local_count, first_half, 0)
    whole_rows(1)

    def second_half(e, _):
        multiply(1, e)
        activate(e)
        return 0

    lax.fori_loop(0, local_count, second_half, 0)

    def cp_a(c):
        return pltpu.make_async_remote_copy(
            src_ref=send_a.at[c],
            dst_ref=recv_a.at[c],
            send_sem=a_ssem.at[c],
            recv_sem=a_rsem.at[c],
            device_id=dp_peer(1, 0),
            device_id_type=MESH,
        )

    def cp_x(c, dx):
        return pltpu.make_async_remote_copy(
            src_ref=send_x.at[c, dx - 1],
            dst_ref=recv_x.at[c, dx - 1],
            send_sem=x_ssem.at[c, dx - 1],
            recv_sem=x_rsem.at[c, dx - 1],
            device_id=dp_peer(0, dx),
            device_id_type=MESH,
        )

    def cp_z(c, dz):
        return pltpu.make_async_remote_copy(
            src_ref=send_z.at[c, dz],
            dst_ref=recv_z.at[c, dz],
            send_sem=z_ssem.at[c, dz],
            recv_sem=z_rsem.at[c, dz],
            device_id=z_peer(dz),
            device_id_type=MESH,
        )

    def project(c):
        down_copy(c).wait()
        down = down_buf[c].reshape(local_count * ff, CHUNK)
        y = jnp.dot(hidden[...], down, preferred_element_type=f32)
        send_a[c] = y[half:].astype(bf16)
        cp_a(c).start()
        own_a[c] = y[:half]

    def add_core(c):
        cp_a(c).wait_recv()
        for dx in range(1, n_x):
            at = slice(dx * chip_rows, (dx + 1) * chip_rows)
            send_x[c, dx - 1] = (own_a[c, at] + recv_a[c, at].astype(f32)).astype(bf16)
            cp_x(c, dx).start()
        own_a[c, :chip_rows] += recv_a[c, :chip_rows].astype(f32)

    def add_x(c):
        y = own_a[c, :chip_rows]
        for dx in range(1, n_x):
            cp_x(c, dx).wait_recv()
            y += recv_x[c, dx - 1].astype(f32)
        for dz in range(n_z):
            cut = y[dz * tok : (dz + 1) * tok]
            cut = [cut[:, g * piece : (g + 1) * piece] for g in range(groups)]
            send_z[c, dz] = jnp.concatenate(cut, axis=0).astype(bf16)
        for dz in order:
            cp_z(c, dz).start()

    def finish(c):
        y = send_z[c, 0].astype(f32)
        for dz in range(1, n_z):
            cp_z(c, dz).wait_recv()
            y += recv_z[c, dz].astype(f32)
        for g in range(groups):
            at = pl.multiple_of(c * CHUNK + g * piece, LANES)
            out[:, pl.ds(at, piece)] = y[g * tok : (g + 1) * tok].astype(bf16)

    def step(i, _):
        for lag, stage in zip(LAGS, (project, add_core, add_x, finish)):

            @pl.when((i >= lag) & (i < count + lag))
            def _():
                stage(i - lag)

        return 0

    lax.fori_loop(0, count + LAGS[-1], step, 0)

    for h in range(HALVES):
        for dz in range(n_z):
            if dz:
                gz(h, dz).wait_send()
            for dx in range(n_x):
                if dx:
                    gx(h, dx, dz).wait_send()
                gc(h, dx, dz).wait_send()

    def drain(c, _):
        cp_a(c).wait_send()
        for dx in range(1, n_x):
            cp_x(c, dx).wait_send()
        for dz in range(1, n_z):
            cp_z(c, dz).wait_send()
        return 0

    lax.fori_loop(0, count, drain, 0)


def body(
    tokens,
    routes,
    combine_weight,
    live_rows,
    gate_projection_weight,
    up_projection_weight,
    down_projection_weight,
):
    f32, bf16 = jnp.float32, jnp.bfloat16
    tok, width = tokens.shape
    top = routes.shape[1]
    n_dp = lax.axis_size("dp")
    n_z = lax.axis_size("expert")
    n_x = n_dp // 2
    local_count, _, ff = gate_projection_weight.shape
    groups = SLAB // tok
    deep = width // HALVES
    part = deep // groups
    count = width // CHUNK
    piece = CHUNK // groups
    chip_rows = n_z * tok
    half = n_x * chip_rows
    total = 2 * half
    depth = min(4, HALVES * local_count)
    vmem = pl.BlockSpec(memory_space=pltpu.VMEM)
    hbm = pl.BlockSpec(memory_space=pl.ANY)
    sem = pltpu.SemaphoreType.DMA
    weights = 3 * local_count * width * ff
    return pl.pallas_call(
        functools.partial(kernel, n_x, n_z, depth),
        out_shape=jax.ShapeDtypeStruct((tok, width), bf16),
        in_specs=[hbm] * 7,
        out_specs=vmem,
        scratch_shapes=[
            pltpu.VMEM((tok, width), bf16),
            pltpu.VMEM((tok, top), jnp.int32),
            pltpu.VMEM((tok, top), bf16),
            pltpu.VMEM((1, 1), jnp.int32),
            pltpu.VMEM((total * groups, part + LANES), bf16),
            pltpu.VMEM((total * groups, part), bf16),
            pltpu.VMEM((HALVES, total, deep), bf16),
            pltpu.VMEM((total, LANES), f32),
            pltpu.VMEM((total, local_count * ff), bf16),
            pltpu.VMEM((local_count, 2, total, ff), f32),
            pltpu.VMEM((depth, 2, BITES, deep // BITES, ff), bf16),
            pltpu.VMEM((count, local_count, ff, CHUNK), bf16),
            pltpu.VMEM((count, half, CHUNK), f32),
            pltpu.VMEM((count, half, CHUNK), bf16),
            pltpu.VMEM((count, half, CHUNK), bf16),
            pltpu.VMEM((count, n_x - 1, chip_rows, CHUNK), bf16),
            pltpu.VMEM((count, n_x - 1, chip_rows, CHUNK), bf16),
            pltpu.VMEM((count, n_z, SLAB, piece), bf16),
            pltpu.VMEM((count, n_z, SLAB, piece), bf16),
            sem((4,)),
            sem((depth, 2, BITES)),
            sem((count,)),
            sem((HALVES, n_z)),
            sem((HALVES, n_z)),
            sem((HALVES, n_x, n_z)),
            sem((HALVES, n_x, n_z)),
            sem((HALVES, n_x, n_z)),
            sem((HALVES, n_x, n_z)),
            sem((count,)),
            sem((count,)),
            sem((count, n_x - 1)),
            sem((count, n_x - 1)),
            sem((count, n_z)),
            sem((count, n_z)),
        ],
        compiler_params=pltpu.CompilerParams(
            collective_id=0, has_side_effects=True, vmem_limit_bytes=64 * 1024 * 1024 - 65536
        ),
        cost_estimate=pl.CostEstimate(
            flops=2 * total * weights, bytes_accessed=2 * weights, transcendentals=total * ff * local_count
        ),
    )(
        tokens,
        routes,
        combine_weight,
        live_rows.reshape(1, 1),
        gate_projection_weight,
        up_projection_weight,
        down_projection_weight,
    )


def solution(mesh):
    placed = (
        P(("groups", "expert", "dp"), None),
        P(("groups", "expert", "dp"), None),
        P(("groups", "expert", "dp"), None),
        P(("groups", "expert", "dp")),
        P("expert", None, "dp"),
        P("expert", None, "dp"),
        P("expert", "dp", None),
    )
    return jax.shard_map(
        body,
        mesh=mesh,
        in_specs=placed,
        out_specs=P(("groups", "expert", "dp"), None),
        check_vma=False,
    )
```
